32 devices in a mesh: prow: 4 (over x, core), pcol: 8 (over z, y).
Axes of the slice: x: 2, y: 2, z: 4, core: 2. Of those that a mesh axis runs over, the one named last changes fastest.
Arguments:
- ancestor_inverse: float32 [2048, 2048], P('prow', 'pcol'), may hold values from -6 to 6
- block_mask: int32 [8, 8], replicated, may hold values 0 or 1
- block_ids: int32 [8], replicated, may hold values from 0 to 7, each once
- row_lists: int32 [4, 4], replicated, may hold values from 0 to 7, as said below
- panels: float32 [2048, 512], P(('prow', 'pcol')), may hold values from -0.21875 to 0.21875
- diag_inverse: float32 [4, 128, 128], replicated, may hold values from -6 to 6
Outputs:
- inverse_panels: float32 [2048, 512], P(('prow', 'pcol'))
- diag_blocks: float32 [4, 128, 128], replicated
The draws below stay inside these ranges and needn't reach their ends.
Inputs may be any that keep to these rules, and one draw needn't show every extreme that they name: `row_lists`: each row names 4 different ancestor blocks.
All inputs are finite; a program needn't handle non-finite values.
Results may differ from the reference program's by a relative error of at most 0.0003.
Values sent between devices are 32-bit elements; how exact they have to be, the bound alone decides.
A program may use at most 64 MiB of HBM per device.

```python
import jax
import jax.numpy as jnp
from jax import lax

BLK = 256
W = 128
S = 4
NB = 8
ORDER = 2048
NR = 4


def draw_row_lists(key, part):
    supernode_keys = jax.random.split(jax.random.fold_in(key, 7), S)

    def choose(one_key):
        return jax.random.permutation(one_key, NB)[:NR].astype(jnp.int32)
    return jax.vmap(choose)(supernode_keys)


def with_ends(array, stream_key, low, largest):
    longest = array.shape.index(max(array.shape))
    spots = []
    for shift in (0, 1):
        where = [jax.random.randint(jax.random.fold_in(stream_key, axis), (), 0, length) for axis, length in enumerate(array.shape)]
        where[longest] = (where[longest] + shift) % array.shape[longest]
        spots.append(tuple(where))
    return array.at[spots[0]].set(low).at[spots[1]].set(largest)


def level_of(own_key, shape, shards, least, largest):
    gain = 1.0
    for dim, blocks in shards:
        heights = jax.random.uniform(jax.random.fold_in(jax.random.fold_in(own_key, 6), dim), (blocks,), jnp.float32, least / len(shards), largest / len(shards))
        gain = gain * jnp.repeat(jnp.exp(heights), shape[dim] // blocks).reshape((-1,) + (1,) * (len(shape) - 1 - dim))
    return gain


def gaussian(key, dims, width, limit, cuts=(), held_as=jnp.bfloat16):
    values = width * jax.random.normal(key, dims, jnp.float32)
    if cuts:
        values = values * level_of(key, dims, cuts, -0.22, 0.18)
    return jnp.clip(values, -limit, limit).astype(held_as)


def setup_inputs(seed: int = 0) -> dict:
    keys = jax.random.split(jax.random.key(seed), 7)
    ancestor_inverse = gaussian(keys[0], (ORDER, ORDER), 1.0, 6.0, ((0, 4), (1, 8)), jnp.float32)
    block_mask = with_ends((jax.random.randint(keys[1], (NB, NB), 0, 4) < 3).astype(jnp.int32), jax.random.fold_in(keys[1], 1), 0, 1)
    block_ids = jax.random.permutation(keys[2], NB).astype(jnp.int32)
    row_lists = draw_row_lists(jax.random.fold_in(keys[6], 71), 0)
    panels = gaussian(keys[4], (ORDER, S * W), (NR * BLK * 3 // 4) ** -0.5, 0.21875, ((0, 32),), jnp.float32)
    diag_inverse = gaussian(keys[5], (S, W, W), 1.0, 6.0, (), jnp.float32)
    return dict(ancestor_inverse=ancestor_inverse, block_mask=block_mask, block_ids=block_ids, row_lists=row_lists, panels=panels, diag_inverse=diag_inverse)


def reference(ancestor_inverse, block_mask, block_ids, row_lists, panels, diag_inverse):
    active_blocks = jnp.any(block_ids[:, None, None] == row_lists[None, :, :], axis=2).astype(jnp.float32)
    row_keep = jnp.repeat(jnp.repeat(active_blocks, BLK, axis=0), W, axis=1)
    active = panels * row_keep
    mask_f = block_mask.astype(jnp.float32)

    def one_block(block_index):
        block_rows = lax.dynamic_slice_in_dim(ancestor_inverse, (block_index * BLK).astype(jnp.int32), BLK, 0)
        keep_cols = jnp.repeat(mask_f[block_index], BLK)
        return jnp.dot(block_rows * keep_cols[None, :], active, precision=lax.Precision.HIGHEST, preferred_element_type=jnp.float32)

    summed = lax.map(one_block, jnp.arange(NB, dtype=jnp.int32)).reshape(NB * BLK, S * W)
    inverse_panels = -(row_keep * summed)
    diag_blocks = diag_inverse - jnp.einsum("isa,isb->sab", active.reshape(-1, S, W), inverse_panels.reshape(-1, S, W), precision=lax.Precision.HIGHEST)
    return inverse_panels, diag_blocks
```

```python
import functools
import itertools

import jax
import jax.numpy as jnp
from jax import lax
from jax.experimental import pallas as pl
from jax.experimental.pallas import tpu as pltpu
from jax.sharding import PartitionSpec as P

BLK = 256
W = 128
S = 4
CHUNKS = 4
CORES = 2
MESH = pl.DeviceIdType.MESH


def halves(value):
    high = value.astype(jnp.bfloat16)
    low = (value - high.astype(jnp.float32)).astype(jnp.bfloat16)
    return high, low


def dot3(a_high, a_low, b_high, b_low):
    dot = functools.partial(jnp.dot, preferred_element_type=jnp.float32)
    return dot(a_high, b_low) + dot(a_low, b_high) + dot(a_high, b_high)


def fused(
    rows_n,
    cols_n,
    block_mask,
    block_ids,
    row_lists,
    ancestor,
    panels,
    diag_inverse,
    panels_out,
    diag_out,
    act,
    far_cols,
    a_high,
    a_low,
    needed,
    partial,
    arrived,
    diag_local,
    diag_near,
    diag_line,
    diag_all,
    sem_a,
    send_1,
    recv_1,
    send_2,
    recv_2,
    sem_3,
    send_c,
    recv_c,
    send_d1,
    recv_d1,
    send_d2,
    recv_d2,
    send_d3,
    recv_d3,
):
    r = lax.axis_index("prow")
    c = lax.axis_index("pcol")
    q = c // 2
    h = c % 2
    x = r // CORES
    core = r % CORES
    far_h = 1 - h
    m = panels.shape[0]
    piece = m // rows_n
    row_span = rows_n * 2 * m
    chunks = act.shape[0]
    per_chunk = S // chunks
    plane = rows_n * 2
    nr = row_lists.shape[1]

    barrier = pltpu.get_barrier_semaphore()
    total = rows_n * cols_n
    flat = r * cols_n + c
    for step in range(1, total):
        other = lax.rem(flat + step, total)
        pl.semaphore_signal(
            barrier, inc=1, device_id=(other // cols_n, other % cols_n), device_id_type=MESH
        )

    def active(block, k):
        hit = block_ids[block] == row_lists[k, 0]
        for n in range(1, nr):
            hit = jnp.logical_or(hit, block_ids[block] == row_lists[k, n])
        return jnp.where(hit, 1.0, 0.0).astype(jnp.float32)

    own_block = (flat * m) // BLK
    keep = [active(own_block, k) for k in range(S)]
    for k in range(S):
        g, i = divmod(k, per_chunk)
        act[g, :, i * W : (i + 1) * W] = panels[:, k * W : (k + 1) * W] * keep[k]

    pl.semaphore_wait(barrier, total - 1)

    def remote(src, dst, send, recv, device):
        return pltpu.make_async_remote_copy(
            src_ref=src, dst_ref=dst, send_sem=send, recv_sem=recv, device_id=device, device_id_type=MESH
        )

    pending = []

    def first(g, j):
        to = lax.rem(r + j, rows_n)
        return remote(
            act.at[g, pl.ds(to * piece, piece)],
            needed.at[g, q, h, to // CORES, to % CORES],
            send_1.at[g, j],
            recv_1.at[g, q],
            (to, r * 2 + h),
        )

    for g in range(chunks):
        for j in range(1, rows_n):
            copy = first(g, j)
            copy.start()
            pending.append(copy)

        @pl.when(q != r)
        def _():
            first(g, 0).start()

        @pl.when(q == r)
        def _():
            needed[g, q, h, x, core] = act[g, pl.ds(r * piece, piece)]

    swap = remote(ancestor.at[:, far_h], far_cols, sem_a.at[0], sem_a.at[1], (r, 2 * q + far_h))
    swap.start()
    pending.append(swap)

    near_steps = [(dx, dh) for dx in range(rows_n // CORES) for dh in range(2)][1:]
    plane_steps = [(dr, dh) for dr in range(rows_n) for dh in range(2)][1:]
    copies = {}

    def split_rows(source, slot, column):
        for to in range(rows_n):
            block = (r * row_span + (2 * to + h) * m) // BLK
            keep_block = block_mask[block, column].astype(jnp.float32)
            high, low = halves(source[to] * keep_block)
            a_high[slot, to * m : (to + 1) * m] = high
            a_low[slot, to * m : (to + 1) * m] = low

    def second(g):
        for source in range(rows_n):
            wait = remote(
                act.at[g, pl.ds(0, piece)],
                needed.at[g, source, h, x, core],
                send_1.at[g, 0],
                recv_1.at[g, source],
                (r, c),
            )

            @pl.when(jnp.logical_or(q != source, r != source))
            def _():
                wait.wait_recv()

        for j, (dx, dh) in enumerate(near_steps):
            to_x = lax.rem(x + dx, rows_n // CORES)
            to_h = lax.rem(h + dh, 2)
            block = needed.at[g, :, h, x, core]
            copy = remote(
                block, block, send_2.at[g, j], recv_2.at[g, j], (to_x * CORES + core, 2 * q + to_h)
            )
            copy.start()
            pending.append(copy)
            copies["second", g, j] = copy

    def third(g):
        for j, (dx, dh) in enumerate(near_steps):
            from_x = lax.rem(x - dx + rows_n // CORES, rows_n // CORES)
            from_h = lax.rem(h - dh + 2, 2)
            block = needed.at[g, :, from_h, from_x, core]
            remote(block, block, send_2.at[g, j], recv_2.at[g, j], (r, c)).wait_recv()
        block = needed.at[g, :, :, :, core]
        copy = remote(
            block, block, sem_3.at[0, g], sem_3.at[1, g], (x * CORES + 1 - core, c)
        )
        copy.start()
        pending.append(copy)

    def multiply(g):
        if g == 0:
            split_rows([ancestor[to, h] for to in range(rows_n)], h, c)
            swap.wait_recv()
            split_rows([far_cols[to] for to in range(rows_n)], far_h, 2 * q + far_h)
        block = needed.at[g, :, :, :, 1 - core]
        remote(block, block, sem_3.at[0, g], sem_3.at[1, g], (r, c)).wait_recv()
        value = None
        width = per_chunk * W
        for side in range(2):
            half = rows_n // 2
            b_high, b_low = halves(
                needed[g, side * half : (side + 1) * half].reshape(half * 2 * m, width)
            )
            term = dot3(a_high[side], a_low[side], b_high, b_low)
            value = term if value is None else value + term
        partial[g] = value.reshape(rows_n, m, width)
        for j in range(1, rows_n):
            to = lax.rem(q + j, rows_n)
            copy = remote(
                partial.at[g, to],
                arrived.at[g, j - 1],
                send_c.at[g, j - 1],
                recv_c.at[g, j - 1],
                (r, 2 * to + h),
            )
            copy.start()
            pending.append(copy)
            copies["line", g, j] = copy

    def finish(g):
        summed = partial[g, q]
        for j in range(1, rows_n):
            copies["line", g, j].wait_recv()
            summed = summed + arrived[g, j - 1]
        for i in range(per_chunk):
            k = g * per_chunk + i
            cols = slice(i * W, (i + 1) * W)
            inverse = -(keep[k] * summed[:, cols])
            panels_out[:, k * W : (k + 1) * W] = inverse
            t_high, t_low = halves(act[g, :, cols].T)
            i_high, i_low = halves(inverse)
            diag_local[g, :, i] = dot3(t_high, t_low, i_high, i_low).reshape(plane, W // plane, W)
        for j, (dr, dh) in enumerate(plane_steps):
            to_r = lax.rem(r + dr, rows_n)
            to_h = lax.rem(h + dh, 2)
            copy = remote(
                diag_local.at[g, to_r * 2 + to_h],
                diag_near.at[g, j],
                send_d1.at[g, j],
                recv_d1.at[g, j],
                (to_r, 2 * q + to_h),
            )
            copy.start()
            pending.append(copy)
            copies["d1", g, j] = copy

    mine = r * 2 + h

    def line_sum(g):
        value = diag_local[g, mine]
        for j in range(plane - 1):
            copies["d1", g, j].wait_recv()
            value = value + diag_near[g, j]
        diag_line[g, q] = value
        for j in range(1, rows_n):
            to = lax.rem(q + j, rows_n)
            copy = remote(
                diag_line.at[g, q],
                diag_line.at[g, q],
                send_d2.at[g, j - 1],
                recv_d2.at[g, j - 1],
                (r, 2 * to + h),
            )
            copy.start()
            pending.append(copy)

    def spread(g):
        for j in range(1, rows_n):
            source = lax.rem(q - j + rows_n, rows_n)
            remote(
                diag_line.at[g, source],
                diag_line.at[g, source],
                send_d2.at[g, j - 1],
                recv_d2.at[g, j - 1],
                (r, c),
            ).wait_recv()
        value = diag_line[g, 0]
        for source in range(1, rows_n):
            value = value + diag_line[g, source]
        share = W // plane
        for i in range(per_chunk):
            k = g * per_chunk + i
            diag_all[g, mine, i] = diag_inverse[k, pl.ds(mine * share, share)] - value[i]
        for j, (dr, dh) in enumerate(plane_steps):
            to_r = lax.rem(r + dr, rows_n)
            to_h = lax.rem(h + dh, 2)
            copy = remote(
                diag_all.at[g, mine],
                diag_all.at[g, mine],
                send_d3.at[g, j],
                recv_d3.at[g, j],
                (to_r, 2 * q + to_h),
            )
            copy.start()
            pending.append(copy)

    def store(g):
        for j, (dr, dh) in enumerate(plane_steps):
            source = lax.rem(r - dr + rows_n, rows_n) * 2 + lax.rem(h - dh + 2, 2)
            remote(
                diag_all.at[g, source],
                diag_all.at[g, source],
                send_d3.at[g, j],
                recv_d3.at[g, j],
                (r, c),
            ).wait_recv()
        for i in range(per_chunk):
            diag_out[g * per_chunk + i] = diag_all[g, :, i].reshape(W, W)

    stages = [second, third, multiply, finish, line_sum, spread, store]
    for turn in range(chunks + len(stages) - 1):
        for depth, stage in enumerate(stages):
            if 0 <= turn - depth < chunks:
                stage(turn - depth)

    for copy in pending:
        copy.wait_send()
    for g in range(chunks):

        @pl.when(q != r)
        def _():
            first(g, 0).wait_send()


def planned(ancestor_inverse, block_mask, block_ids, row_lists, panels, diag_inverse):
    rows_n = lax.axis_size("prow")
    cols_n = lax.axis_size("pcol")
    m = panels.shape[0]
    col_span = ancestor_inverse.shape[1]
    g = CHUNKS
    width = S // g * W
    plane = 2 * rows_n
    piece = m // rows_n
    share = W // plane
    f32 = jnp.float32
    dma = pltpu.SemaphoreType.DMA
    vmem = pl.BlockSpec(memory_space=pltpu.VMEM)
    smem = pl.BlockSpec(memory_space=pltpu.SMEM)
    return pl.pallas_call(
        functools.partial(fused, rows_n, cols_n),
        out_shape=(
            jax.ShapeDtypeStruct(panels.shape, f32),
            jax.ShapeDtypeStruct(diag_inverse.shape, f32),
        ),
        in_specs=[smem, smem, smem, vmem, vmem, vmem],
        out_specs=(vmem, vmem),
        scratch_shapes=[
            pltpu.VMEM((g, m, width), f32),
            pltpu.VMEM((rows_n, m, col_span), f32),
            pltpu.VMEM((2, rows_n * m, col_span), jnp.bfloat16),
            pltpu.VMEM((2, rows_n * m, col_span), jnp.bfloat16),
            pltpu.VMEM((g, rows_n, 2, rows_n // CORES, CORES, piece, width), f32),
            pltpu.VMEM((g, rows_n, m, width), f32),
            pltpu.VMEM((g, rows_n - 1, m, width), f32),
            pltpu.VMEM((g, plane, S // g, share, W), f32),
            pltpu.VMEM((g, plane - 1, S // g, share, W), f32),
            pltpu.VMEM((g, rows_n, S // g, share, W), f32),
            pltpu.VMEM((g, plane, S // g, share, W), f32),
            dma((2,)),
            dma((g, rows_n)),
            dma((g, rows_n)),
            dma((g, rows_n - 1)),
            dma((g, rows_n - 1)),
            dma((2, g)),
            dma((g, rows_n - 1)),
            dma((g, rows_n - 1)),
            dma((g, plane - 1)),
            dma((g, plane - 1)),
            dma((g, rows_n - 1)),
            dma((g, rows_n - 1)),
            dma((g, plane - 1)),
            dma((g, plane - 1)),
        ],
        compiler_params=pltpu.CompilerParams(
            collective_id=0, has_side_effects=True, vmem_limit_bytes=32 * 1024 * 1024
        ),
    )(
        block_mask,
        block_ids,
        row_lists,
        ancestor_inverse.reshape(rows_n, 2, m, col_span),
        panels,
        diag_inverse,
    )


def from_partner(block, axis, stride):
    count = lax.axis_size(axis)
    route = []
    for low in range(count):
        high = low | 1 << stride
        if high != low and high < count:
            route += [(low, high), (high, low)]
    return lax.ppermute(block, axis, route)


def general(ancestor_inverse, block_mask, block_ids, row_lists, panels, diag_inverse):
    row_devices = lax.axis_size("prow")
    col_devices = lax.axis_size("pcol")
    prow_index = lax.axis_index("prow")
    pcol_index = lax.axis_index("pcol")
    row_count = panels.shape[0]
    block_total = block_ids.shape[0]
    panel_width = S * W
    row_span = ancestor_inverse.shape[0]
    col_span = ancestor_inverse.shape[1]
    active_blocks = jnp.any(block_ids[:, None, None] == row_lists[None, :, :], axis=2).astype(
        jnp.float32
    )
    flat_index = prow_index * col_devices + pcol_index
    own_rows = flat_index * row_count + jnp.arange(row_count, dtype=jnp.int32)
    picker = (own_rows[:, None] // BLK == jnp.arange(block_total, dtype=jnp.int32)[None, :]).astype(
        jnp.float32
    )
    own_keep = jnp.repeat(
        jnp.dot(picker, active_blocks, preferred_element_type=jnp.float32), W, axis=1
    )
    active_own = panels * own_keep
    half_rows = row_count // 2
    upper_part = active_own[:half_rows]
    lower_part = active_own[half_rows:]
    in_first = pcol_index // row_devices == 0
    kept_part = jnp.where(in_first, upper_part, lower_part)
    given_part = jnp.where(in_first, lower_part, upper_part)
    pair_bit = row_devices.bit_length() - 1
    partner_part = from_partner(given_part, "pcol", pair_bit)
    stacked = jnp.stack([kept_part, partner_part])[None]
    colset = lax.all_gather(stacked, "prow", axis=0, tiled=True)
    send_slots = jnp.where(in_first, colset, colset[:, ::-1]).reshape(
        col_devices, half_rows, panel_width
    )
    arrived = lax.all_to_all(send_slots, "pcol", split_axis=0, concat_axis=0, tiled=True)
    needed = jnp.concatenate([arrived[:row_devices], arrived[row_devices:]], axis=1).reshape(
        col_span, panel_width
    )
    block_rows = row_span // BLK
    block_cols = col_span // BLK
    local_mask = lax.dynamic_slice(
        block_mask, (prow_index * block_rows, pcol_index * block_cols), (block_rows, block_cols)
    ).astype(jnp.float32)
    masked_local = (
        ancestor_inverse.reshape(block_rows, BLK, block_cols, BLK) * local_mask[:, None, :, None]
    ).reshape(row_span, col_span)
    partial_value = jnp.dot(
        masked_local, needed, precision=lax.Precision.HIGHEST, preferred_element_type=jnp.float32
    )
    summed = lax.psum_scatter(partial_value, "pcol", scatter_dimension=0, tiled=True)
    inverse_panels = -(own_keep * summed)
    local_diag = jnp.einsum(
        "isa,isb->sab",
        active_own.reshape(row_count, S, W),
        inverse_panels.reshape(row_count, S, W),
        precision=lax.Precision.HIGHEST,
    )
    diag_total = lax.psum(local_diag, ("prow", "pcol"))
    return (inverse_panels, diag_inverse - diag_total)


def local(ancestor_inverse, block_mask, block_ids, row_lists, panels, diag_inverse):
    rows_n = lax.axis_size("prow")
    cols_n = lax.axis_size("pcol")
    m = panels.shape[0]
    fits = (
        cols_n == 2 * rows_n
        and rows_n % CORES == 0
        and m % (8 * rows_n) == 0
        and BLK % m == 0
        and ancestor_inverse.shape[1] == BLK
        and W % (16 * rows_n) == 0
    )
    plan = planned if fits else general
    return plan(ancestor_inverse, block_mask, block_ids, row_lists, panels, diag_inverse)


def solution(mesh):
    placed = (P("prow", "pcol"), P(), P(), P(), P(("prow", "pcol"), None), P())
    return jax.shard_map(
        local,
        mesh=mesh,
        in_specs=placed,
        out_specs=(P(("prow", "pcol"), None), P()),
        check_vma=False,
    )
```

```python
import functools

import jax
import jax.numpy as jnp
from jax import lax
from jax.experimental import pallas as pl
from jax.experimental.pallas import tpu as pltpu
from jax.sharding import PartitionSpec as P

BLK = 256
W = 128
S = 4
CHUNKS = 2
CORES = 2
MESH = pl.DeviceIdType.MESH


def halves(value):
    high = value.astype(jnp.bfloat16)
    low = (value - high.astype(jnp.float32)).astype(jnp.bfloat16)
    return high, low


def dot3(a_high, a_low, b_high, b_low):
    dot = functools.partial(jnp.dot, preferred_element_type=jnp.float32)
    return dot(a_high, b_low) + dot(a_low, b_high) + dot(a_high, b_high)


def fused(
    rows_n,
    cols_n,
    mask_hbm,
    ids_hbm,
    lists_hbm,
    ancestor,
    panels_hbm,
    diag_hbm,
    panels_out,
    diag_out,
    block_mask,
    block_ids,
    row_lists,
    near_cols,
    panels,
    diag_inverse,
    sem_in,
    act,
    far_cols,
    a_high,
    a_low,
    needed,
    partial,
    arrived,
    diag_local,
    diag_near,
    diag_line,
    diag_all,
    sem_a,
    send_1,
    recv_1,
    send_2,
    recv_2,
    sem_3,
    send_c,
    recv_c,
    send_d1,
    recv_d1,
    send_d2,
    recv_d2,
    send_d3,
    recv_d3,
):
    r = lax.axis_index("prow")
    c = lax.axis_index("pcol")
    q = c // 2
    h = c % 2
    x = r // CORES
    core = r % CORES
    far_h = 1 - h
    m = panels.shape[0]
    piece = m // rows_n
    row_span = rows_n * 2 * m
    chunks = act.shape[0]
    per_chunk = S // chunks
    plane = rows_n * 2
    nr = row_lists.shape[1]

    share = W // plane
    mine = r * 2 + h
    loads = [
        pltpu.make_async_copy(src, dst, sem_in.at[i])
        for i, (src, dst) in enumerate(
            [
                (panels_hbm, panels),
                (ids_hbm, block_ids),
                (lists_hbm, row_lists),
                (mask_hbm, block_mask),
                (ancestor.at[:, h], near_cols),
                (diag_hbm.at[:, pl.ds(mine * share, share)], diag_inverse),
            ]
        )
    ]
    for load in loads:
        load.start()

    barrier = pltpu.get_barrier_semaphore()
    total = rows_n * cols_n
    flat = r * cols_n + c
    for step in range(1, total):
        other = lax.rem(flat + step, total)
        pl.semaphore_signal(
            barrier, inc=1, device_id=(other // cols_n, other % cols_n), device_id_type=MESH
        )

    def active(block, k):
        hit = block_ids[block] == row_lists[k, 0]
        for n in range(1, nr):
            hit = jnp.logical_or(hit, block_ids[block] == row_lists[k, n])
        return jnp.where(hit, 1.0, 0.0).astype(jnp.float32)

    for load in loads[:4]:
        load.wait()
    own_block = (flat * m) // BLK
    keep = [active(own_block, k) for k in range(S)]
    for k in range(S):
        g, i = divmod(k, per_chunk)
        act[g, :, i * W : (i + 1) * W] = panels[:, k * W : (k + 1) * W] * keep[k]

    pl.semaphore_wait(barrier, total - 1)

    def remote(src, dst, send, recv, device):
        return pltpu.make_async_remote_copy(
            src_ref=src, dst_ref=dst, send_sem=send, recv_sem=recv, device_id=device, device_id_type=MESH
        )

    pending = []

    def first(g, j):
        to = lax.rem(r + j, rows_n)
        return remote(
            act.at[g, pl.ds(to * piece, piece)],
            needed.at[g, q, h, to // CORES, to % CORES],
            send_1.at[g, j],
            recv_1.at[g, q],
            (to, r * 2 + h),
        )

    for g in range(chunks):
        for j in range(1, rows_n):
            copy = first(g, j)
            copy.start()
            pending.append(copy)

        @pl.when(q != r)
        def _():
            first(g, 0).start()

        @pl.when(q == r)
        def _():
            needed[g, q, h, x, core] = act[g, pl.ds(r * piece, piece)]

    swap = remote(ancestor.at[:, far_h], far_cols, sem_a.at[0], sem_a.at[1], (r, 2 * q + far_h))
    swap.start()
    pending.append(swap)

    near_steps = [(dx, dh) for dx in range(rows_n // CORES) for dh in range(2)][1:]
    plane_steps = [(dr, dh) for dr in range(rows_n) for dh in range(2)][1:]
    copies = {}

    def split_rows(source, slot, column):
        for to in range(rows_n):
            block = (r * row_span + (2 * to + h) * m) // BLK
            keep_block = block_mask[block, column].astype(jnp.float32)
            high, low = halves(source[to] * keep_block)
            a_high[slot, to * m : (to + 1) * m] = high
            a_low[slot, to * m : (to + 1) * m] = low

    def second(g):
        for source in range(rows_n):
            wait = remote(
                act.at[g, pl.ds(0, piece)],
                needed.at[g, source, h, x, core],
                send_1.at[g, 0],
                recv_1.at[g, source],
                (r, c),
            )

            @pl.when(jnp.logical_or(q != source, r != source))
            def _():
                wait.wait_recv()

        for j, (dx, dh) in enumerate(near_steps):
            to_x = lax.rem(x + dx, rows_n // CORES)
            to_h = lax.rem(h + dh, 2)
            block = needed.at[g, :, h, x, core]
            copy = remote(
                block, block, send_2.at[g, j], recv_2.at[g, j], (to_x * CORES + core, 2 * q + to_h)
            )
            copy.start()
            pending.append(copy)
            copies["second", g, j] = copy

    def third(g):
        for j, (dx, dh) in enumerate(near_steps):
            from_x = lax.rem(x - dx + rows_n // CORES, rows_n // CORES)
            from_h = lax.rem(h - dh + 2, 2)
            block = needed.at[g, :, from_h, from_x, core]
            remote(block, block, send_2.at[g, j], recv_2.at[g, j], (r, c)).wait_recv()
        block = needed.at[g, :, :, :, core]
        copy = remote(
            block, block, sem_3.at[0, g], sem_3.at[1, g], (x * CORES + 1 - core, c)
        )
        copy.start()
        pending.append(copy)

    def multiply(g):
        if g == 0:
            loads[4].wait()
            split_rows([near_cols[to] for to in range(rows_n)], h, c)
            swap.wait_recv()
            split_rows([far_cols[to] for to in range(rows_n)], far_h, 2 * q + far_h)
        block = needed.at[g, :, :, :, 1 - core]
        remote(block, block, sem_3.at[0, g], sem_3.at[1, g], (r, c)).wait_recv()
        value = None
        width = per_chunk * W
        for side in range(2):
            half = rows_n // 2
            b_high, b_low = halves(
                needed[g, side * half : (side + 1) * half].reshape(half * 2 * m, width)
            )
            term = dot3(a_high[side], a_low[side], b_high, b_low)
            value = term if value is None else value + term
        partial[g] = value.reshape(rows_n, m, width)
        for j in range(1, rows_n):
            to = lax.rem(q + j, rows_n)
            copy = remote(
                partial.at[g, to],
                arrived.at[g, j - 1],
                send_c.at[g, j - 1],
                recv_c.at[g, j - 1],
                (r, 2 * to + h),
            )
            copy.start()
            pending.append(copy)
            copies["line", g, j] = copy

    def finish(g):
        summed = partial[g, q]
        for j in range(1, rows_n):
            copies["line", g, j].wait_recv()
            summed = summed + arrived[g, j - 1]
        for i in range(per_chunk):
            k = g * per_chunk + i
            cols = slice(i * W, (i + 1) * W)
            inverse = -(keep[k] * summed[:, cols])
            panels_out[:, k * W : (k + 1) * W] = inverse
            t_high, t_low = halves(act[g, :, cols].T)
            i_high, i_low = halves(inverse)
            diag_local[g, :, i] = dot3(t_high, t_low, i_high, i_low).reshape(plane, W // plane, W)
        for j, (dr, dh) in enumerate(plane_steps):
            to_r = lax.rem(r + dr, rows_n)
            to_h = lax.rem(h + dh, 2)
            copy = remote(
                diag_local.at[g, to_r * 2 + to_h],
                diag_near.at[g, j],
                send_d1.at[g, j],
                recv_d1.at[g, j],
                (to_r, 2 * q + to_h),
            )
            copy.start()
            pending.append(copy)
            copies["d1", g, j] = copy

    def line_sum(g):
        value = diag_local[g, mine]
        for j in range(plane - 1):
            copies["d1", g, j].wait_recv()
            value = value + diag_near[g, j]
        diag_line[g, q] = value
        for j in range(1, rows_n):
            to = lax.rem(q + j, rows_n)
            copy = remote(
                diag_line.at[g, q],
                diag_line.at[g, q],
                send_d2.at[g, j - 1],
                recv_d2.at[g, j - 1],
                (r, 2 * to + h),
            )
            copy.start()
            pending.append(copy)

    def spread(g):
        for j in range(1, rows_n):
            source = lax.rem(q - j + rows_n, rows_n)
            remote(
                diag_line.at[g, source],
                diag_line.at[g, source],
                send_d2.at[g, j - 1],
                recv_d2.at[g, j - 1],
                (r, c),
            ).wait_recv()
        value = diag_line[g, 0]
        for source in range(1, rows_n):
            value = value + diag_line[g, source]
        if g == 0:
            loads[5].wait()
        for i in range(per_chunk):
            diag_all[g, mine, i] = diag_inverse[g * per_chunk + i] - value[i]
        for j, (dr, dh) in enumerate(plane_steps):
            to_r = lax.rem(r + dr, rows_n)
            to_h = lax.rem(h + dh, 2)
            copy = remote(
                diag_all.at[g, mine],
                diag_all.at[g, mine],
                send_d3.at[g, j],
                recv_d3.at[g, j],
                (to_r, 2 * q + to_h),
            )
            copy.start()
            pending.append(copy)

    def store(g):
        for j, (dr, dh) in enumerate(plane_steps):
            source = lax.rem(r - dr + rows_n, rows_n) * 2 + lax.rem(h - dh + 2, 2)
            remote(
                diag_all.at[g, source],
                diag_all.at[g, source],
                send_d3.at[g, j],
                recv_d3.at[g, j],
                (r, c),
            ).wait_recv()
        for i in range(per_chunk):
            diag_out[g * per_chunk + i] = diag_all[g, :, i].reshape(W, W)

    stages = [second, third, multiply, finish, line_sum, spread, store]
    for turn in range(chunks + len(stages) - 1):
        for depth, stage in enumerate(stages):
            if 0 <= turn - depth < chunks:
                stage(turn - depth)

    for copy in pending:
        copy.wait_send()
    for g in range(chunks):

        @pl.when(q != r)
        def _():
            first(g, 0).wait_send()


def planned(ancestor_inverse, block_mask, block_ids, row_lists, panels, diag_inverse):
    rows_n = lax.axis_size("prow")
    cols_n = lax.axis_size("pcol")
    m = panels.shape[0]
    col_span = ancestor_inverse.shape[1]
    g = CHUNKS
    width = S // g * W
    plane = 2 * rows_n
    piece = m // rows_n
    share = W // plane
    f32 = jnp.float32
    dma = pltpu.SemaphoreType.DMA
    vmem = pl.BlockSpec(memory_space=pltpu.VMEM)
    anywhere = pl.BlockSpec(memory_space=pl.ANY)
    return pl.pallas_call(
        functools.partial(fused, rows_n, cols_n),
        out_shape=(
            jax.ShapeDtypeStruct(panels.shape, f32),
            jax.ShapeDtypeStruct(diag_inverse.shape, f32),
        ),
        in_specs=[anywhere] * 6,
        out_specs=(vmem, vmem),
        scratch_shapes=[
            pltpu.SMEM(block_mask.shape, jnp.int32),
            pltpu.SMEM(block_ids.shape, jnp.int32),
            pltpu.SMEM(row_lists.shape, jnp.int32),
            pltpu.VMEM((rows_n, m, col_span), f32),
            pltpu.VMEM(panels.shape, f32),
            pltpu.VMEM((S, share, W), f32),
            dma((6,)),
            pltpu.VMEM((g, m, width), f32),
            pltpu.VMEM((rows_n, m, col_span), f32),
            pltpu.VMEM((2, rows_n * m, col_span), jnp.bfloat16),
            pltpu.VMEM((2, rows_n * m, col_span), jnp.bfloat16),
            pltpu.VMEM((g, rows_n, 2, rows_n // CORES, CORES, piece, width), f32),
            pltpu.VMEM((g, rows_n, m, width), f32),
            pltpu.VMEM((g, rows_n - 1, m, width), f32),
            pltpu.VMEM((g, plane, S // g, share, W), f32),
            pltpu.VMEM((g, plane - 1, S // g, share, W), f32),
            pltpu.VMEM((g, rows_n, S // g, share, W), f32),
            pltpu.VMEM((g, plane, S // g, share, W), f32),
            dma((2,)),
            dma((g, rows_n)),
            dma((g, rows_n)),
            dma((g, rows_n - 1)),
            dma((g, rows_n - 1)),
            dma((2, g)),
            dma((g, rows_n - 1)),
            dma((g, rows_n - 1)),
            dma((g, plane - 1)),
            dma((g, plane - 1)),
            dma((g, rows_n - 1)),
            dma((g, rows_n - 1)),
            dma((g, plane - 1)),
            dma((g, plane - 1)),
        ],
        compiler_params=pltpu.CompilerParams(
            collective_id=0, has_side_effects=True, vmem_limit_bytes=60 * 1024 * 1024
        ),
    )(
        block_mask,
        block_ids,
        row_lists,
        ancestor_inverse.reshape(rows_n, 2, m, col_span),
        panels,
        diag_inverse,
    )


def from_partner(block, axis, stride):
    count = lax.axis_size(axis)
    route = []
    for low in range(count):
        high = low | 1 << stride
        if high != low and high < count:
            route += [(low, high), (high, low)]
    return lax.ppermute(block, axis, route)


def general(ancestor_inverse, block_mask, block_ids, row_lists, panels, diag_inverse):
    row_devices = lax.axis_size("prow")
    col_devices = lax.axis_size("pcol")
    prow_index = lax.axis_index("prow")
    pcol_index = lax.axis_index("pcol")
    row_count = panels.shape[0]
    block_total = block_ids.shape[0]
    panel_width = S * W
    row_span = ancestor_inverse.shape[0]
    col_span = ancestor_inverse.shape[1]
    active_blocks = jnp.any(block_ids[:, None, None] == row_lists[None, :, :], axis=2).astype(
        jnp.float32
    )
    flat_index = prow_index * col_devices + pcol_index
    own_rows = flat_index * row_count + jnp.arange(row_count, dtype=jnp.int32)
    picker = (own_rows[:, None] // BLK == jnp.arange(block_total, dtype=jnp.int32)[None, :]).astype(
        jnp.float32
    )
    own_keep = jnp.repeat(
        jnp.dot(picker, active_blocks, preferred_element_type=jnp.float32), W, axis=1
    )
    active_own = panels * own_keep
    half_rows = row_count // 2
    upper_part = active_own[:half_rows]
    lower_part = active_own[half_rows:]
    in_first = pcol_index // row_devices == 0
    kept_part = jnp.where(in_first, upper_part, lower_part)
    given_part = jnp.where(in_first, lower_part, upper_part)
    pair_bit = row_devices.bit_length() - 1
    partner_part = from_partner(given_part, "pcol", pair_bit)
    stacked = jnp.stack([kept_part, partner_part])[None]
    colset = lax.all_gather(stacked, "prow", axis=0, tiled=True)
    send_slots = jnp.where(in_first, colset, colset[:, ::-1]).reshape(
        col_devices, half_rows, panel_width
    )
    arrived = lax.all_to_all(send_slots, "pcol", split_axis=0, concat_axis=0, tiled=True)
    needed = jnp.concatenate([arrived[:row_devices], arrived[row_devices:]], axis=1).reshape(
        col_span, panel_width
    )
    block_rows = row_span // BLK
    block_cols = col_span // BLK
    local_mask = lax.dynamic_slice(
        block_mask, (prow_index * block_rows, pcol_index * block_cols), (block_rows, block_cols)
    ).astype(jnp.float32)
    masked_local = (
        ancestor_inverse.reshape(block_rows, BLK, block_cols, BLK) * local_mask[:, None, :, None]
    ).reshape(row_span, col_span)
    partial_value = jnp.dot(
        masked_local, needed, precision=lax.Precision.HIGHEST, preferred_element_type=jnp.float32
    )
    summed = lax.psum_scatter(partial_value, "pcol", scatter_dimension=0, tiled=True)
    inverse_panels = -(own_keep * summed)
    local_diag = jnp.einsum(
        "isa,isb->sab",
        active_own.reshape(row_count, S, W),
        inverse_panels.reshape(row_count, S, W),
        precision=lax.Precision.HIGHEST,
    )
    diag_total = lax.psum(local_diag, ("prow", "pcol"))
    return (inverse_panels, diag_inverse - diag_total)


def local(ancestor_inverse, block_mask, block_ids, row_lists, panels, diag_inverse):
    rows_n = lax.axis_size("prow")
    cols_n = lax.axis_size("pcol")
    m = panels.shape[0]
    fits = (
        cols_n == 2 * rows_n
        and rows_n % CORES == 0
        and m % (8 * rows_n) == 0
        and BLK % m == 0
        and ancestor_inverse.shape[1] == BLK
        and W % (16 * rows_n) == 0
    )
    plan = planned if fits else general
    return plan(ancestor_inverse, block_mask, block_ids, row_lists, panels, diag_inverse)


def solution(mesh):
    placed = (P("prow", "pcol"), P(), P(), P(), P(("prow", "pcol"), None), P())
    return jax.shard_map(
        local,
        mesh=mesh,
        in_specs=placed,
        out_specs=(P(("prow", "pcol"), None), P()),
        check_vma=False,
    )
```

```python
import functools

import jax
import jax.numpy as jnp
from jax import lax
from jax.experimental import pallas as pl
from jax.experimental.pallas import tpu as pltpu
from jax.sharding import PartitionSpec as P

BLK = 256
W = 128
S = 4
CHUNKS = 2
CORES = 2
MESH = pl.DeviceIdType.MESH


def halves(value):
    high = value.astype(jnp.bfloat16)
    low = (value - high.astype(jnp.float32)).astype(jnp.bfloat16)
    return high, low


def dot3(a_high, a_low, b_high, b_low):
    dot = functools.partial(jnp.dot, preferred_element_type=jnp.float32)
    return dot(a_high, b_low) + dot(a_low, b_high) + dot(a_high, b_high)


def fused(
    rows_n,
    cols_n,
    mask_hbm,
    ids_hbm,
    lists_hbm,
    ancestor,
    panels_hbm,
    diag_hbm,
    panels_out,
    diag_out,
    block_mask,
    block_ids,
    row_lists,
    near_cols,
    panels,
    diag_inverse,
    sem_in,
    act,
    far_cols,
    a_high,
    a_low,
    needed,
    partial,
    arrived,
    diag_local,
    diag_near,
    diag_line,
    diag_all,
    sem_a,
    send_1,
    recv_1,
    send_2,
    recv_2,
    sem_3,
    send_c,
    recv_c,
    send_d1,
    recv_d1,
    send_d2,
    recv_d2,
    send_d3,
    recv_d3,
):
    r = lax.axis_index("prow")
    c = lax.axis_index("pcol")
    q = c // 2
    h = c % 2
    x = r // CORES
    core = r % CORES
    far_h = 1 - h
    m = panels.shape[0]
    piece = m // rows_n
    row_span = rows_n * 2 * m
    chunks = act.shape[0]
    per_chunk = S // chunks
    plane = rows_n * 2
    nr = row_lists.shape[1]

    share = W // plane
    mine = r * 2 + h
    loads = [
        pltpu.make_async_copy(src, dst, sem_in.at[i])
        for i, (src, dst) in enumerate(
            [
                (panels_hbm, panels),
                (ids_hbm, block_ids),
                (lists_hbm, row_lists),
                (mask_hbm, block_mask),
                (ancestor.at[:, h], near_cols),
                (diag_hbm.at[:, pl.ds(mine * share, share)], diag_inverse),
            ]
        )
    ]
    for load in loads:
        load.start()

    barrier = pltpu.get_barrier_semaphore()
    flat = r * cols_n + c
    near_steps = [(dx, dh) for dx in range(rows_n // CORES) for dh in range(2)][1:]
    plane_steps = [(dr, dh) for dr in range(rows_n) for dh in range(2)][1:]

    def greet(to_r, to_q, to_h):
        pl.semaphore_signal(
            barrier, inc=1, device_id=(to_r, 2 * to_q + to_h), device_id_type=MESH
        )

    for dr, dh in plane_steps:
        greet(lax.rem(r + dr, rows_n), q, lax.rem(h + dh, 2))
    for step in range(1, rows_n):
        greet(r, lax.rem(q + step, rows_n), h)
    apart = q != r

    @pl.when(apart)
    def _():
        for step in range(1, rows_n):
            greet(lax.rem(r + step, rows_n), r, h)
            source = lax.rem(q + step, rows_n)

            @pl.when(source != r)
            def _():
                greet(q, source, h)

    def active(block, k):
        hit = block_ids[block] == row_lists[k, 0]
        for n in range(1, nr):
            hit = jnp.logical_or(hit, block_ids[block] == row_lists[k, n])
        return jnp.where(hit, 1.0, 0.0).astype(jnp.float32)

    for load in loads[:4]:
        load.wait()
    own_block = (flat * m) // BLK
    keep = [active(own_block, k) for k in range(S)]
    for k in range(S):
        g, i = divmod(k, per_chunk)
        act[g, :, i * W : (i + 1) * W] = panels[:, k * W : (k + 1) * W] * keep[k]

    met = plane - 1 + rows_n - 1
    pl.semaphore_wait(barrier, jnp.where(apart, met + 2 * rows_n - 3, met))

    def remote(src, dst, send, recv, device):
        return pltpu.make_async_remote_copy(
            src_ref=src, dst_ref=dst, send_sem=send, recv_sem=recv, device_id=device, device_id_type=MESH
        )

    pending = []

    def first(g, j):
        to = lax.rem(r + j, rows_n)
        return remote(
            act.at[g, pl.ds(to * piece, piece)],
            needed.at[g, q, h, to // CORES, to % CORES],
            send_1.at[g, j],
            recv_1.at[g, q],
            (to, r * 2 + h),
        )

    for g in range(chunks):
        for j in range(1, rows_n):
            copy = first(g, j)
            copy.start()
            pending.append(copy)

        @pl.when(q != r)
        def _():
            first(g, 0).start()

        @pl.when(q == r)
        def _():
            needed[g, q, h, x, core] = act[g, pl.ds(r * piece, piece)]

    swap = remote(ancestor.at[:, far_h], far_cols, sem_a.at[0], sem_a.at[1], (r, 2 * q + far_h))
    swap.start()
    pending.append(swap)

    copies = {}

    def split_rows(source, slot, column):
        for to in range(rows_n):
            block = (r * row_span + (2 * to + h) * m) // BLK
            keep_block = block_mask[block, column].astype(jnp.float32)
            high, low = halves(source[to] * keep_block)
            a_high[slot, to * m : (to + 1) * m] = high
            a_low[slot, to * m : (to + 1) * m] = low

    loads[4].wait()
    split_rows([near_cols[to] for to in range(rows_n)], h, c)

    def second(g):
        for source in range(rows_n):
            wait = remote(
                act.at[g, pl.ds(0, piece)],
                needed.at[g, source, h, x, core],
                send_1.at[g, 0],
                recv_1.at[g, source],
                (r, c),
            )

            @pl.when(jnp.logical_or(q != source, r != source))
            def _():
                wait.wait_recv()

        for j, (dx, dh) in enumerate(near_steps):
            to_x = lax.rem(x + dx, rows_n // CORES)
            to_h = lax.rem(h + dh, 2)
            block = needed.at[g, :, h, x, core]
            copy = remote(
                block, block, send_2.at[g, j], recv_2.at[g, j], (to_x * CORES + core, 2 * q + to_h)
            )
            copy.start()
            pending.append(copy)
            copies["second", g, j] = copy

    def third(g):
        for j, (dx, dh) in enumerate(near_steps):
            from_x = lax.rem(x - dx + rows_n // CORES, rows_n // CORES)
            from_h = lax.rem(h - dh + 2, 2)
            block = needed.at[g, :, from_h, from_x, core]
            remote(block, block, send_2.at[g, j], recv_2.at[g, j], (r, c)).wait_recv()
        block = needed.at[g, :, :, :, core]
        copy = remote(
            block, block, sem_3.at[0, g], sem_3.at[1, g], (x * CORES + 1 - core, c)
        )
        copy.start()
        pending.append(copy)

    def multiply(g):
        if g == 0:
            swap.wait_recv()
            split_rows([far_cols[to] for to in range(rows_n)], far_h, 2 * q + far_h)
        block = needed.at[g, :, :, :, 1 - core]
        remote(block, block, sem_3.at[0, g], sem_3.at[1, g], (r, c)).wait_recv()
        value = None
        width = per_chunk * W
        for side in range(2):
            half = rows_n // 2
            b_high, b_low = halves(
                needed[g, side * half : (side + 1) * half].reshape(half * 2 * m, width)
            )
            term = dot3(a_high[side], a_low[side], b_high, b_low)
            value = term if value is None else value + term
        partial[g] = value.reshape(rows_n, m, width)
        for j in range(1, rows_n):
            to = lax.rem(q + j, rows_n)
            copy = remote(
                partial.at[g, to],
                arrived.at[g, j - 1],
                send_c.at[g, j - 1],
                recv_c.at[g, j - 1],
                (r, 2 * to + h),
            )
            copy.start()
            pending.append(copy)
            copies["line", g, j] = copy

    def finish(g):
        summed = partial[g, q]
        for j in range(1, rows_n):
            copies["line", g, j].wait_recv()
            summed = summed + arrived[g, j - 1]
        for i in range(per_chunk):
            k = g * per_chunk + i
            cols = slice(i * W, (i + 1) * W)
            inverse = -(keep[k] * summed[:, cols])
            panels_out[:, k * W : (k + 1) * W] = inverse
            t_high, t_low = halves(act[g, :, cols].T)
            i_high, i_low = halves(inverse)
            diag_local[g, :, i] = dot3(t_high, t_low, i_high, i_low).reshape(plane, W // plane, W)
        for j, (dr, dh) in enumerate(plane_steps):
            to_r = lax.rem(r + dr, rows_n)
            to_h = lax.rem(h + dh, 2)
            copy = remote(
                diag_local.at[g, to_r * 2 + to_h],
                diag_near.at[g, j],
                send_d1.at[g, j],
                recv_d1.at[g, j],
                (to_r, 2 * q + to_h),
            )
            copy.start()
            pending.append(copy)
            copies["d1", g, j] = copy

    def line_sum(g):
        value = diag_local[g, mine]
        for j in range(plane - 1):
            copies["d1", g, j].wait_recv()
            value = value + diag_near[g, j]
        diag_line[g, q] = value
        for j in range(1, rows_n):
            to = lax.rem(q + j, rows_n)
            copy = remote(
                diag_line.at[g, q],
                diag_line.at[g, q],
                send_d2.at[g, j - 1],
                recv_d2.at[g, j - 1],
                (r, 2 * to + h),
            )
            copy.start()
            pending.append(copy)

    def spread(g):
        for j in range(1, rows_n):
            source = lax.rem(q - j + rows_n, rows_n)
            remote(
                diag_line.at[g, source],
                diag_line.at[g, source],
                send_d2.at[g, j - 1],
                recv_d2.at[g, j - 1],
                (r, c),
            ).wait_recv()
        value = diag_line[g, 0]
        for source in range(1, rows_n):
            value = value + diag_line[g, source]
        if g == 0:
            loads[5].wait()
        for i in range(per_chunk):
            diag_all[g, mine, i] = diag_inverse[g * per_chunk + i] - value[i]
        for j, (dr, dh) in enumerate(plane_steps):
            to_r = lax.rem(r + dr, rows_n)
            to_h = lax.rem(h + dh, 2)
            copy = remote(
                diag_all.at[g, mine],
                diag_all.at[g, mine],
                send_d3.at[g, j],
                recv_d3.at[g, j],
                (to_r, 2 * q + to_h),
            )
            copy.start()
            pending.append(copy)

    def store(g):
        for j, (dr, dh) in enumerate(plane_steps):
            source = lax.rem(r - dr + rows_n, rows_n) * 2 + lax.rem(h - dh + 2, 2)
            remote(
                diag_all.at[g, source],
                diag_all.at[g, source],
                send_d3.at[g, j],
                recv_d3.at[g, j],
                (r, c),
            ).wait_recv()
        for i in range(per_chunk):
            diag_out[g * per_chunk + i] = diag_all[g, :, i].reshape(W, W)

    stages = [second, third, multiply, finish, line_sum, spread, store]
    for turn in range(chunks + len(stages) - 1):
        for depth, stage in enumerate(stages):
            if 0 <= turn - depth < chunks:
                stage(turn - depth)

    for copy in pending:
        copy.wait_send()
    for g in range(chunks):

        @pl.when(q != r)
        def _():
            first(g, 0).wait_send()


def planned(ancestor_inverse, block_mask, block_ids, row_lists, panels, diag_inverse):
    rows_n = lax.axis_size("prow")
    cols_n = lax.axis_size("pcol")
    m = panels.shape[0]
    col_span = ancestor_inverse.shape[1]
    g = CHUNKS
    width = S // g * W
    plane = 2 * rows_n
    piece = m // rows_n
    share = W // plane
    f32 = jnp.float32
    dma = pltpu.SemaphoreType.DMA
    vmem = pl.BlockSpec(memory_space=pltpu.VMEM)
    anywhere = pl.BlockSpec(memory_space=pl.ANY)
    return pl.pallas_call(
        functools.partial(fused, rows_n, cols_n),
        out_shape=(
            jax.ShapeDtypeStruct(panels.shape, f32),
            jax.ShapeDtypeStruct(diag_inverse.shape, f32),
        ),
        in_specs=[anywhere] * 6,
        out_specs=(vmem, vmem),
        scratch_shapes=[
            pltpu.SMEM(block_mask.shape, jnp.int32),
            pltpu.SMEM(block_ids.shape, jnp.int32),
            pltpu.SMEM(row_lists.shape, jnp.int32),
            pltpu.VMEM((rows_n, m, col_span), f32),
            pltpu.VMEM(panels.shape, f32),
            pltpu.VMEM((S, share, W), f32),
            dma((6,)),
            pltpu.VMEM((g, m, width), f32),
            pltpu.VMEM((rows_n, m, col_span), f32),
            pltpu.VMEM((2, rows_n * m, col_span), jnp.bfloat16),
            pltpu.VMEM((2, rows_n * m, col_span), jnp.bfloat16),
            pltpu.VMEM((g, rows_n, 2, rows_n // CORES, CORES, piece, width), f32),
            pltpu.VMEM((g, rows_n, m, width), f32),
            pltpu.VMEM((g, rows_n - 1, m, width), f32),
            pltpu.VMEM((g, plane, S // g, share, W), f32),
            pltpu.VMEM((g, plane - 1, S // g, share, W), f32),
            pltpu.VMEM((g, rows_n, S // g, share, W), f32),
            pltpu.VMEM((g, plane, S // g, share, W), f32),
            dma((2,)),
            dma((g, rows_n)),
            dma((g, rows_n)),
            dma((g, rows_n - 1)),
            dma((g, rows_n - 1)),
            dma((2, g)),
            dma((g, rows_n - 1)),
            dma((g, rows_n - 1)),
            dma((g, plane - 1)),
            dma((g, plane - 1)),
            dma((g, rows_n - 1)),
            dma((g, rows_n - 1)),
            dma((g, plane - 1)),
            dma((g, plane - 1)),
        ],
        compiler_params=pltpu.CompilerParams(
            collective_id=0, has_side_effects=True, vmem_limit_bytes=60 * 1024 * 1024
        ),
    )(
        block_mask,
        block_ids,
        row_lists,
        ancestor_inverse.reshape(rows_n, 2, m, col_span),
        panels,
        diag_inverse,
    )


def from_partner(block, axis, stride):
    count = lax.axis_size(axis)
    route = []
    for low in range(count):
        high = low | 1 << stride
        if high != low and high < count:
            route += [(low, high), (high, low)]
    return lax.ppermute(block, axis, route)


def general(ancestor_inverse, block_mask, block_ids, row_lists, panels, diag_inverse):
    row_devices = lax.axis_size("prow")
    col_devices = lax.axis_size("pcol")
    prow_index = lax.axis_index("prow")
    pcol_index = lax.axis_index("pcol")
    row_count = panels.shape[0]
    block_total = block_ids.shape[0]
    panel_width = S * W
    row_span = ancestor_inverse.shape[0]
    col_span = ancestor_inverse.shape[1]
    active_blocks = jnp.any(block_ids[:, None, None] == row_lists[None, :, :], axis=2).astype(
        jnp.float32
    )
    flat_index = prow_index * col_devices + pcol_index
    own_rows = flat_index * row_count + jnp.arange(row_count, dtype=jnp.int32)
    picker = (own_rows[:, None] // BLK == jnp.arange(block_total, dtype=jnp.int32)[None, :]).astype(
        jnp.float32
    )
    own_keep = jnp.repeat(
        jnp.dot(picker, active_blocks, preferred_element_type=jnp.float32), W, axis=1
    )
    active_own = panels * own_keep
    half_rows = row_count // 2
    upper_part = active_own[:half_rows]
    lower_part = active_own[half_rows:]
    in_first = pcol_index // row_devices == 0
    kept_part = jnp.where(in_first, upper_part, lower_part)
    given_part = jnp.where(in_first, lower_part, upper_part)
    pair_bit = row_devices.bit_length() - 1
    partner_part = from_partner(given_part, "pcol", pair_bit)
    stacked = jnp.stack([kept_part, partner_part])[None]
    colset = lax.all_gather(stacked, "prow", axis=0, tiled=True)
    send_slots = jnp.where(in_first, colset, colset[:, ::-1]).reshape(
        col_devices, half_rows, panel_width
    )
    arrived = lax.all_to_all(send_slots, "pcol", split_axis=0, concat_axis=0, tiled=True)
    needed = jnp.concatenate([arrived[:row_devices], arrived[row_devices:]], axis=1).reshape(
        col_span, panel_width
    )
    block_rows = row_span // BLK
    block_cols = col_span // BLK
    local_mask = lax.dynamic_slice(
        block_mask, (prow_index * block_rows, pcol_index * block_cols), (block_rows, block_cols)
    ).astype(jnp.float32)
    masked_local = (
        ancestor_inverse.reshape(block_rows, BLK, block_cols, BLK) * local_mask[:, None, :, None]
    ).reshape(row_span, col_span)
    partial_value = jnp.dot(
        masked_local, needed, precision=lax.Precision.HIGHEST, preferred_element_type=jnp.float32
    )
    summed = lax.psum_scatter(partial_value, "pcol", scatter_dimension=0, tiled=True)
    inverse_panels = -(own_keep * summed)
    local_diag = jnp.einsum(
        "isa,isb->sab",
        active_own.reshape(row_count, S, W),
        inverse_panels.reshape(row_count, S, W),
        precision=lax.Precision.HIGHEST,
    )
    diag_total = lax.psum(local_diag, ("prow", "pcol"))
    return (inverse_panels, diag_inverse - diag_total)


def local(ancestor_inverse, block_mask, block_ids, row_lists, panels, diag_inverse):
    rows_n = lax.axis_size("prow")
    cols_n = lax.axis_size("pcol")
    m = panels.shape[0]
    fits = (
        cols_n == 2 * rows_n
        and rows_n % CORES == 0
        and m % (8 * rows_n) == 0
        and BLK % m == 0
        and ancestor_inverse.shape[1] == BLK
        and W % (16 * rows_n) == 0
    )
    plan = planned if fits else general
    return plan(ancestor_inverse, block_mask, block_ids, row_lists, panels, diag_inverse)


def solution(mesh):
    placed = (P("prow", "pcol"), P(), P(), P(), P(("prow", "pcol"), None), P())
    return jax.shard_map(
        local,
        mesh=mesh,
        in_specs=placed,
        out_specs=(P(("prow", "pcol"), None), P()),
        check_vma=False,
    )
```
